32 devices in a mesh: var: 8 (over y, x, core), smp: 4 (over z).
Axes of the slice: x: 2, y: 2, z: 4, core: 2. Of those that a mesh axis runs over, the one named last changes fastest.
Arguments:
- dosages: bfloat16 [8192, 16384], P('var', 'smp'), may hold values from 0 to 2
- window_end: int32 [8192], P('var'), may hold values from 1 to 8192, as said below
Outputs:
- ld_band: float32 [8192, 512], P('var', 'smp')
The draws below stay inside these ranges and needn't reach their ends.
Inputs may be any that keep to these rules, and one draw needn't show every extreme that they name: Nondecreasing along the variants; window_end[i] > i and window_end[i] - i - 1 <= 512, with equality for some variants of every draw; never past 8192.
All inputs are finite; a program needn't handle non-finite values.
Results may differ from the reference program's by a relative error of at most 0.0003.
Values may be sent and summed in bfloat16 or wider, within the bound.
A program may use at most 128 MiB of HBM per device.

```python
import jax
import jax.numpy as jnp
from jax import lax

WIN = 512
VARIANTS = 8192
SAMPLES = 16384
REGION = 256


def draw_dosages(key, part):
    key = jax.random.fold_in(key, 11)
    key_shared, key_noise, key_load, key_offset, key_grade = jax.random.split(key, 5)
    region_count = VARIANTS // REGION
    loading = jax.random.uniform(key_load, (VARIANTS,), jnp.float32, 0.6, 1.4)
    offsets = jax.random.uniform(key_offset, (VARIANTS,), jnp.float32, -2.0, 1.0)
    gradient = jax.random.uniform(key_grade, (VARIANTS,), jnp.float32, -1.0, 1.0)
    drift = (jnp.arange(SAMPLES, dtype=jnp.float32) + 0.5) / SAMPLES - 0.5
    fraction = (jnp.arange(REGION, dtype=jnp.float32) + 0.5) / REGION

    def one_region(region_index):
        first = jax.random.normal(jax.random.fold_in(key_shared, region_index), (SAMPLES,), jnp.float32)
        second = jax.random.normal(jax.random.fold_in(key_shared, region_index + 1), (SAMPLES,), jnp.float32)
        begin = region_index * REGION
        load_rows = lax.dynamic_slice_in_dim(loading, begin, REGION)
        offset_rows = lax.dynamic_slice_in_dim(offsets, begin, REGION)
        grade_rows = lax.dynamic_slice_in_dim(gradient, begin, REGION)
        shared = jnp.sqrt(1.0 - fraction)[:, None] * first[None, :] + jnp.sqrt(fraction)[:, None] * second[None, :]
        noise_key = jax.random.fold_in(key_noise, region_index)
        noise = 0.7 * jax.random.normal(noise_key, (REGION, SAMPLES), jnp.float32)
        latent = load_rows[:, None] * shared + noise + 1.5 * grade_rows[:, None] * drift[None, :]
        values = 2.0 / (1.0 + jnp.exp(-(offset_rows[:, None] + 0.8 * latent)))
        return values.astype(jnp.bfloat16)
    regions = lax.map(one_region, jnp.arange(region_count, dtype=jnp.int32))
    return regions.reshape(VARIANTS, SAMPLES)


def draw_window_end(key, part):
    key = jax.random.fold_in(key, 7)
    key_scale, key_step = jax.random.split(key)
    region_count = VARIANTS // (2 * WIN)
    scales = jax.random.randint(key_scale, (region_count,), 1, 9)
    scales = jnp.where(jnp.arange(region_count) == 0, 1, scales)
    per_variant = jnp.repeat(scales, 2 * WIN)
    steps_raw = jax.random.randint(key_step, (VARIANTS,), 0, 1 << 20)
    steps_taken = steps_raw % (2 * per_variant) + 1
    position = jnp.cumsum(steps_taken).astype(jnp.int32)
    reach = jnp.searchsorted(position, position + 2 * WIN + 1, side='left').astype(jnp.int32)
    limit = jnp.arange(VARIANTS, dtype=jnp.int32) + 1 + WIN
    return jnp.minimum(reach, limit).astype(jnp.int32)


def setup_inputs(seed: int = 0) -> dict:
    keys = jax.random.split(jax.random.key(seed), 3)
    dosages = draw_dosages(jax.random.fold_in(keys[2], 71), 0)
    window_end = draw_window_end(jax.random.fold_in(keys[2], 71), 0)
    return {"dosages": dosages, "window_end": window_end}


def standard(block):
    samples = block.shape[1]
    widened = block.astype(jnp.float32)
    average = lax.optimization_barrier(jnp.sum(widened, axis=1)) / samples
    spread = lax.optimization_barrier(jnp.sum(widened * widened, axis=1)) / samples - average * average
    return ((widened - average[:, None]) * lax.rsqrt(spread + 1e-06)[:, None]).astype(jnp.bfloat16)

def skewed(product, width):
    flattened = jnp.pad(product.reshape(-1), (0, width + 1))
    return flattened[1:1 + width * (2 * width + 1)].reshape(width, 2 * width + 1)[:, :width]

def reference(dosages, window_end):
    variants, samples = dosages.shape
    block_count = variants // WIN
    scaled = lax.map(standard, dosages.reshape(block_count, WIN, samples))
    following = jnp.concatenate([scaled[1:], jnp.zeros((1, WIN, samples), jnp.bfloat16)], axis=0)

    def one_block(items):
        current, after = items
        left = current.astype(jnp.float32)
        right = jnp.concatenate([current, after], axis=0).astype(jnp.float32)
        product = jnp.dot(left, right.T, precision=lax.Precision.HIGHEST, preferred_element_type=jnp.float32)
        return skewed(product, WIN)
    banded = lax.map(one_block, (scaled, following)).reshape(variants, WIN)
    row_index = jnp.arange(variants, dtype=jnp.int32)
    column = jnp.arange(WIN, dtype=jnp.int32)
    retain = column[None, :] < (window_end - row_index - 1)[:, None]
    return jnp.where(retain, banded / samples, jnp.float32(0.0))
```

```python
import functools

import jax
import jax.numpy as jnp
from jax import lax
from jax.experimental import pallas as pl
from jax.experimental.pallas import tpu as pltpu
from jax.sharding import PartitionSpec as P

WIN = 512
LANE = 128
SUB = 8
SPAN = WIN // LANE
MESH = pl.DeviceIdType.MESH
NT = (((1,), (1,)), ((), ()))


def kernel(
    x_ref, end_ref, out_ref,
    own, after, product, outbox, inbox, moments, moments_in, final, final_after,
    load_sem, after_send, after_recv, moment_send, moment_recv,
    final_send, final_recv, band_send, band_recv,
):
    rows, depth = own.shape
    groups = rows // LANE
    var, smp = lax.axis_index("var"), lax.axis_index("smp")
    var_count, smp_count = lax.axis_size("var"), lax.axis_size("smp")
    samples = depth * smp_count
    has_left, has_right = var > 0, var < var_count - 1

    def peer(step):
        return lax.rem(smp + step, smp_count)

    loads = [
        pltpu.make_async_copy(
            x_ref.at[pl.ds(g * LANE, LANE)], own.at[pl.ds(g * LANE, LANE)], load_sem.at[g]
        )
        for g in range(groups)
    ]
    for load in loads:
        load.start()

    barrier = pltpu.get_barrier_semaphore()
    for step in range(1, smp_count):
        pl.semaphore_signal(barrier, 1, device_id=(var, peer(step)), device_id_type=MESH)

    @pl.when(has_left)
    def _():
        pl.semaphore_signal(barrier, 1, device_id=(var - 1, smp), device_id_type=MESH)

    @pl.when(has_right)
    def _():
        pl.semaphore_signal(barrier, 1, device_id=(var + 1, smp), device_id_type=MESH)

    pl.semaphore_wait(
        barrier, smp_count - 1 + has_left.astype(jnp.int32) + has_right.astype(jnp.int32)
    )

    def after_copy(q):
        return pltpu.make_async_remote_copy(
            src_ref=x_ref.at[pl.ds(q * LANE, LANE)],
            dst_ref=after.at[pl.ds(q * LANE, LANE)],
            send_sem=after_send.at[q],
            recv_sem=after_recv.at[q],
            device_id=(var - 1, smp),
            device_id_type=MESH,
        )

    def final_copy():
        return pltpu.make_async_remote_copy(
            src_ref=final,
            dst_ref=final_after,
            send_sem=final_send,
            recv_sem=final_recv,
            device_id=(var - 1, smp),
            device_id_type=MESH,
        )

    @pl.when(has_left)
    def _():
        for q in range(SPAN):
            after_copy(q).start()

    for g in range(groups):
        loads[g].wait()

        def add(t, sums):
            tile = own[pl.ds(g * LANE, LANE), pl.ds(pl.multiple_of(t * LANE, LANE), LANE)]
            tile = tile.astype(jnp.float32)
            return sums[0] + tile, sums[1] + tile * tile

        zero = jnp.zeros((LANE, LANE), jnp.float32)
        first, second = lax.fori_loop(0, depth // LANE, add, (zero, zero), unroll=4)
        moments[pl.ds(g, 1), :] = jnp.sum(first.T, axis=0, keepdims=True)
        moments[pl.ds(groups + g, 1), :] = jnp.sum(second.T, axis=0, keepdims=True)

    def moment_copy(step):
        return pltpu.make_async_remote_copy(
            src_ref=moments,
            dst_ref=moments_in.at[step - 1],
            send_sem=moment_send.at[step - 1],
            recv_sem=moment_recv.at[step - 1],
            device_id=(var, peer(step)),
            device_id_type=MESH,
        )

    for step in range(1, smp_count):
        moment_copy(step).start()
    for step in range(1, smp_count):
        moment_copy(step).wait()
    total = moments[...]
    for step in range(1, smp_count):
        total = total + moments_in[step - 1]
    average = total[:groups] / samples
    spread = total[groups:] / samples - average * average
    final[pl.ds(0, groups), :] = average
    final[pl.ds(groups, groups), :] = lax.rsqrt(spread + 1e-06)

    @pl.when(has_left)
    def _():
        final_copy().start()

    def column(row):
        return jnp.broadcast_to(row, (LANE, LANE)).T

    def standardize(held, g, stats):
        shift = column(stats[pl.ds(g, 1), :])
        scale = column(stats[pl.ds(groups + g, 1), :])

        @pl.loop(0, depth // LANE, unroll=4)
        def _(t):
            at = (pl.ds(g * LANE, LANE), pl.ds(pl.multiple_of(t * LANE, LANE), LANE))
            held[at] = ((held[at].astype(jnp.float32) - shift) * scale).astype(jnp.bfloat16)

    def band_copy(g, step):
        return pltpu.make_async_remote_copy(
            src_ref=outbox.at[g, peer(step)],
            dst_ref=inbox.at[g, step - 1],
            send_sem=band_send.at[g, step - 1],
            recv_sem=band_recv.at[g, step - 1],
            device_id=(var, peer(step)),
            device_id_type=MESH,
        )

    def finish_group(g):
        width, share = WIN + LANE, WIN // smp_count
        for top in range(0, LANE, SUB):
            value = pltpu.roll(product[g, pl.ds(top, SUB), :], width - 1 - top, 1)
            line = lax.broadcasted_iota(jnp.int32, (SUB, width), 0)
            for bit in range(3):
                moved = pltpu.roll(value, width - (1 << bit), 1)
                value = jnp.where((line >> bit) & 1 == 1, moved, value)
            for part in range(smp_count):
                outbox[g, part, pl.ds(top, SUB), :] = value[:, part * share : (part + 1) * share]
        for step in range(1, smp_count):
            band_copy(g, step).start()

    def place(value, row, col):
        for i in range(value.shape[0] // LANE):
            for j in range(value.shape[1] // LANE):
                g, c = row + i, col + j - row - i
                if 0 <= c <= SPAN:
                    product[g, :, pl.ds(c * LANE, LANE)] = value[
                        i * LANE : (i + 1) * LANE, j * LANE : (j + 1) * LANE
                    ]

    def dot(left, right):
        return lax.dot_general(left, right, NT, preferred_element_type=jnp.float32)

    for g in range(groups):
        standardize(own, g, final)
    for g in range(0, groups, 2):
        for c in range(g, min(g + SPAN + 2, groups), 2):
            value = dot(own[pl.ds(g * LANE, 2 * LANE), :], own[pl.ds(c * LANE, 2 * LANE), :])
            place(value, g, c)
        for done in range(g, g + 2):
            if done + SPAN < groups:
                finish_group(done)

    @pl.when(has_right)
    def _():
        final_copy().wait_recv()

    @pl.when(jnp.logical_not(has_right))
    def _():
        final_after[...] = jnp.zeros_like(final_after)
        after[...] = jnp.zeros_like(after)

    for q in range(SPAN):
        @pl.when(has_right)
        def _():
            after_copy(q).wait_recv()

        standardize(after, q, final_after)
        row = groups - SPAN + q
        value = dot(own[pl.ds(row * LANE, (SPAN - q) * LANE), :], after[pl.ds(q * LANE, LANE), :])
        place(value, row, groups + q)
        finish_group(row)

    lane = lax.broadcasted_iota(jnp.int32, (LANE, LANE), 1)
    line = lax.broadcasted_iota(jnp.int32, (LANE, LANE), 0)
    for g in range(groups):
        for step in range(1, smp_count):
            band_copy(g, step).wait()
        total = outbox[g, smp]
        for step in range(1, smp_count):
            total = total + inbox[g, step - 1]
        end = column(end_ref[pl.ds(g, 1), :].astype(jnp.float32)).astype(jnp.int32)
        index = var * rows + g * LANE + line
        retain = smp * LANE + lane < end - index - 1
        out_ref[pl.ds(g * LANE, LANE), :] = jnp.where(retain, total / samples, 0.0)

    @pl.when(has_left)
    def _():
        final_copy().wait_send()
        for q in range(SPAN):
            after_copy(q).wait_send()


def local(dosages, window_end):
    rows, depth = dosages.shape
    smp_count = lax.axis_size("smp")
    groups = rows // LANE
    share = WIN // smp_count
    dma = pltpu.SemaphoreType.DMA
    return pl.pallas_call(
        kernel,
        out_shape=jax.ShapeDtypeStruct((rows, share), jnp.float32),
        in_specs=[pl.BlockSpec(memory_space=pl.ANY), pl.BlockSpec(memory_space=pltpu.VMEM)],
        out_specs=pl.BlockSpec(memory_space=pltpu.VMEM),
        scratch_shapes=[
            pltpu.VMEM((rows, depth), jnp.bfloat16),
            pltpu.VMEM((WIN, depth), jnp.bfloat16),
            pltpu.VMEM((groups, LANE, WIN + LANE), jnp.float32),
            pltpu.VMEM((groups, smp_count, LANE, share), jnp.float32),
            pltpu.VMEM((groups, smp_count - 1, LANE, share), jnp.float32),
            pltpu.VMEM((2 * groups, LANE), jnp.float32),
            pltpu.VMEM((smp_count - 1, 2 * groups, LANE), jnp.float32),
            pltpu.VMEM((2 * groups, LANE), jnp.float32),
            pltpu.VMEM((2 * groups, LANE), jnp.float32),
            dma((groups,)),
            dma((SPAN,)),
            dma((SPAN,)),
            dma((smp_count - 1,)),
            dma((smp_count - 1,)),
            dma,
            dma,
            dma((groups, smp_count - 1)),
            dma((groups, smp_count - 1)),
        ],
        compiler_params=pltpu.CompilerParams(
            collective_id=0, has_side_effects=True, vmem_limit_bytes=48 * 1024 * 1024
        ),
    )(dosages, window_end.reshape(groups, LANE))


def solution(mesh):
    return jax.shard_map(
        local,
        mesh=mesh,
        in_specs=(P("var", "smp"), P("var")),
        out_specs=P("var", "smp"),
        check_vma=False,
    )
```

```python
import functools

import jax
import jax.numpy as jnp
from jax import lax
from jax.experimental import pallas as pl
from jax.experimental.pallas import tpu as pltpu
from jax.sharding import PartitionSpec as P

WIN = 512
LANE = 128
SUB = 8
SPAN = WIN // LANE
MESH = pl.DeviceIdType.MESH
NT = (((1,), (1,)), ((), ()))


def kernel(
    x_ref, end_ref, out_ref,
    own, after, before, lent, product, outbox, inbox, relayed, moments, moments_in, final, final_after, final_before,
    load_sem, after_send, after_recv, before_send, before_recv, lent_send, lent_recv, moment_send, moment_recv,
    final_send, final_recv, final_send_right, final_recv_right, band_send, band_recv, relay_recv,
):
    rows, depth = own.shape
    groups = rows // LANE
    var, smp = lax.axis_index("var"), lax.axis_index("smp")
    var_count, smp_count = lax.axis_size("var"), lax.axis_size("smp")
    samples = depth * smp_count
    has_left, has_right = var > 0, var < var_count - 1

    def split_of(boundary):
        between_chips = (boundary + 1) // 2 if var_count == 8 else SPAN // 2
        return jnp.where(lax.rem(boundary, 2) == 0, SPAN, between_chips)

    columns_out = jnp.where(has_left, split_of(var - 1), 0)
    rows_in = jnp.where(has_left, split_of(var - 1), SPAN)
    columns_in = jnp.where(has_right, split_of(var), SPAN)
    rows_out = columns_in

    def peer(step):
        return lax.rem(smp + step, smp_count)

    loads = [
        pltpu.make_async_copy(
            x_ref.at[pl.ds(g * LANE, LANE)], own.at[pl.ds(g * LANE, LANE)], load_sem.at[g]
        )
        for g in range(groups)
    ]
    for load in loads:
        load.start()

    barrier = pltpu.get_barrier_semaphore()
    for step in range(1, smp_count):
        pl.semaphore_signal(barrier, 1, device_id=(var, peer(step)), device_id_type=MESH)

    @pl.when(has_left)
    def _():
        pl.semaphore_signal(barrier, 1, device_id=(var - 1, smp), device_id_type=MESH)

    @pl.when(has_right)
    def _():
        pl.semaphore_signal(barrier, 1, device_id=(var + 1, smp), device_id_type=MESH)

    pl.semaphore_wait(
        barrier, smp_count - 1 + has_left.astype(jnp.int32) + has_right.astype(jnp.int32)
    )

    def after_copy(q):
        return pltpu.make_async_remote_copy(
            src_ref=x_ref.at[pl.ds(q * LANE, LANE)],
            dst_ref=after.at[pl.ds(q * LANE, LANE)],
            send_sem=after_send.at[q],
            recv_sem=after_recv.at[q],
            device_id=(var - 1, smp),
            device_id_type=MESH,
        )

    def before_copy(q):
        return pltpu.make_async_remote_copy(
            src_ref=x_ref.at[pl.ds(rows - WIN + q * LANE, LANE)],
            dst_ref=before.at[pl.ds(q * LANE, LANE)],
            send_sem=before_send.at[q],
            recv_sem=before_recv.at[q],
            device_id=(var + 1, smp),
            device_id_type=MESH,
        )

    def lent_copy(q, c):
        return pltpu.make_async_remote_copy(
            src_ref=lent.at[q, c],
            dst_ref=product.at[groups - SPAN + q, :, pl.ds((c + SPAN - q) * LANE, LANE)],
            send_sem=lent_send.at[q, c],
            recv_sem=lent_recv.at[q, c],
            device_id=(var - 1, smp),
            device_id_type=MESH,
        )

    def final_copy():
        return pltpu.make_async_remote_copy(
            src_ref=final,
            dst_ref=final_after,
            send_sem=final_send,
            recv_sem=final_recv,
            device_id=(var - 1, smp),
            device_id_type=MESH,
        )

    def final_copy_right():
        return pltpu.make_async_remote_copy(
            src_ref=final,
            dst_ref=final_before,
            send_sem=final_send_right,
            recv_sem=final_recv_right,
            device_id=(var + 1, smp),
            device_id_type=MESH,
        )

    for q in range(SPAN):
        @pl.when(q < columns_out)
        def _():
            after_copy(q).start()

        @pl.when(q >= rows_out)
        def _():
            before_copy(q).start()

    for g in range(groups):
        loads[g].wait()

        def add(t, sums):
            tile = own[pl.ds(g * LANE, LANE), pl.ds(pl.multiple_of(t * LANE, LANE), LANE)]
            tile = tile.astype(jnp.float32)
            return sums[0] + tile, sums[1] + tile * tile

        zero = jnp.zeros((LANE, LANE), jnp.float32)
        first, second = lax.fori_loop(0, depth // LANE, add, (zero, zero), unroll=4)
        moments[pl.ds(g, 1), :] = jnp.sum(first.T, axis=0, keepdims=True)
        moments[pl.ds(groups + g, 1), :] = jnp.sum(second.T, axis=0, keepdims=True)

    def moment_copy(step):
        return pltpu.make_async_remote_copy(
            src_ref=moments,
            dst_ref=moments_in.at[step - 1],
            send_sem=moment_send.at[step - 1],
            recv_sem=moment_recv.at[step - 1],
            device_id=(var, peer(step)),
            device_id_type=MESH,
        )

    for step in range(1, smp_count):
        moment_copy(step).start()
    for step in range(1, smp_count):
        moment_copy(step).wait()
    total = moments[...]
    for step in range(1, smp_count):
        total = total + moments_in[step - 1]
    average = total[:groups] / samples
    spread = total[groups:] / samples - average * average
    final[pl.ds(0, groups), :] = average
    final[pl.ds(groups, groups), :] = lax.rsqrt(spread + 1e-06)

    @pl.when(has_left)
    def _():
        final_copy().start()

    @pl.when(has_right)
    def _():
        final_copy_right().start()

    def column(row):
        return jnp.broadcast_to(row, (LANE, LANE)).T

    def standardize(held, g, stats, at_stats):
        shift = column(stats[pl.ds(at_stats, 1), :])
        scale = column(stats[pl.ds(groups + at_stats, 1), :])

        @pl.loop(0, depth // LANE, unroll=4)
        def _(t):
            at = (pl.ds(g * LANE, LANE), pl.ds(pl.multiple_of(t * LANE, LANE), LANE))
            held[at] = ((held[at].astype(jnp.float32) - shift) * scale).astype(jnp.bfloat16)

    inward = jnp.where(smp < smp_count // 2, 1, -1)
    at_end = (smp == 0) | (smp == smp_count - 1)
    far = jnp.where(at_end, smp + 3 * inward, smp + 2 * inward)
    second = jnp.where(at_end, smp + 2 * inward, smp - inward)

    def band_copy(g, slot, share, target, landing, recv_sem):
        return pltpu.make_async_remote_copy(
            src_ref=outbox.at[g, share],
            dst_ref=landing,
            send_sem=band_send.at[g, slot],
            recv_sem=recv_sem,
            device_id=(var, target),
            device_id_type=MESH,
        )

    def direct_copy(g, slot, share):
        return band_copy(g, slot, share, share, inbox.at[g, smp], band_recv.at[g, smp])

    def relay_copy(g):
        return band_copy(g, 2, far, smp + inward, relayed.at[g], relay_recv.at[g])

    def arrival(g, sender):
        return band_copy(g, 0, smp, smp + inward, inbox.at[g, sender], band_recv.at[g, sender])

    def relay_group(g):
        @pl.when(jnp.logical_not(at_end))
        def _():
            relay_copy(g).wait_recv()
            outbox[g, far] = outbox[g, far] + relayed[g]
            direct_copy(g, 2, far).start()

    def finish_group(g):
        width, share = WIN + LANE, WIN // smp_count
        for top in range(0, LANE, SUB):
            value = pltpu.roll(product[g, pl.ds(top, SUB), :], width - 1 - top, 1)
            line = lax.broadcasted_iota(jnp.int32, (SUB, width), 0)
            for bit in range(3):
                moved = pltpu.roll(value, width - (1 << bit), 1)
                value = jnp.where((line >> bit) & 1 == 1, moved, value)
            for part in range(smp_count):
                outbox[g, part, pl.ds(top, SUB), :] = value[:, part * share : (part + 1) * share]

        if g == groups - 1:
            direct_copy(g, 2, far).start()
        else:
            @pl.when(at_end)
            def _():
                relay_copy(g).start()

        direct_copy(g, 0, smp + inward).start()
        direct_copy(g, 1, second).start()

    lane = lax.broadcasted_iota(jnp.int32, (LANE, LANE), 1)
    line = lax.broadcasted_iota(jnp.int32, (LANE, LANE), 0)

    def finalize(g):
        arrival(g, smp + inward).wait_recv()
        arrival(g, second).wait_recv()
        outbox[g, smp] = outbox[g, smp] + inbox[g, smp + inward] + inbox[g, second]

        @pl.when(jnp.logical_not(at_end) | (g == groups - 1))
        def _():
            arrival(g, far).wait_recv()
            outbox[g, smp] = outbox[g, smp] + inbox[g, far]

        end = column(end_ref[pl.ds(g, 1), :].astype(jnp.float32)).astype(jnp.int32)
        index = var * rows + g * LANE + line
        retain = smp * LANE + lane < end - index - 1
        out_ref[pl.ds(g * LANE, LANE), :] = jnp.where(retain, outbox[g, smp] / samples, 0.0)

    def place(value, row, col):
        for i in range(value.shape[0] // LANE):
            for j in range(value.shape[1] // LANE):
                g, c = row + i, col + j - row - i
                if 0 <= c <= SPAN:
                    product[g, :, pl.ds(c * LANE, LANE)] = value[
                        i * LANE : (i + 1) * LANE, j * LANE : (j + 1) * LANE
                    ]

    def dot(left, right):
        return lax.dot_general(left, right, NT, preferred_element_type=jnp.float32)

    for g in range(groups):
        standardize(own, g, final, g)
    for g in range(0, groups, 2):
        for c in range(g, min(g + SPAN + 2, groups), 2):
            value = dot(own[pl.ds(g * LANE, 2 * LANE), :], own[pl.ds(c * LANE, 2 * LANE), :])
            place(value, g, c)
        for done in range(g, g + 2):
            if done + SPAN < groups:
                finish_group(done)
                if done > 0:
                    relay_group(done - 1)

    @pl.when(has_right)
    def _():
        final_copy().wait_recv()

    @pl.when(jnp.logical_not(has_right))
    def _():
        final_after[...] = jnp.zeros_like(final_after)
        after[...] = jnp.zeros_like(after)

    for q in range(SPAN):
        row = groups - SPAN + q

        @pl.when(q < columns_in)
        def _():
            @pl.when(has_right)
            def _():
                after_copy(q).wait_recv()

            standardize(after, q, final_after, q)
            left = own[pl.ds(row * LANE, (SPAN - q) * LANE), :]
            place(dot(left, after[pl.ds(q * LANE, LANE), :]), row, groups + q)

        relay_group(row - 1)
        if q >= 2:
            @pl.when(columns_in < SPAN)
            def _():
                finalize(2 * q - 4)
                finalize(2 * q - 3)

        for c in range(q + 1):
            @pl.when(c >= columns_in)
            def _():
                lent_copy(q, c).wait_recv()

        finish_group(row)

    @pl.when(has_left)
    def _():
        final_copy_right().wait_recv()

    for q in range(SPAN):
        @pl.when(q >= rows_in)
        def _():
            before_copy(q).wait_recv()
            standardize(before, q, final_before, groups - SPAN + q)
            value = dot(before[pl.ds(q * LANE, LANE), :], own[pl.ds(0, (q + 1) * LANE), :])
            for c in range(q + 1):
                @pl.when(c >= rows_in)
                def _():
                    lent[q, c] = value[:, c * LANE : (c + 1) * LANE]
                    lent_copy(q, c).start()

    @pl.when(columns_in == SPAN)
    def _():
        for g in range(groups - SPAN):
            finalize(g)

    for g in range(groups - SPAN, groups):
        finalize(g)

    for g in range(groups):
        for slot in range(3):
            band_copy(
                g, slot, far, smp + inward, relayed.at[g], relay_recv.at[g]
            ).wait_send()

    @pl.when(has_left)
    def _():
        final_copy().wait_send()

    @pl.when(has_right)
    def _():
        final_copy_right().wait_send()

    for q in range(SPAN):
        @pl.when(q < columns_out)
        def _():
            after_copy(q).wait_send()

        @pl.when(q >= rows_out)
        def _():
            before_copy(q).wait_send()

        for c in range(q + 1):
            @pl.when((q >= rows_in) & (c >= rows_in))
            def _():
                lent_copy(q, c).wait_send()


def local(dosages, window_end):
    rows, depth = dosages.shape
    smp_count = lax.axis_size("smp")
    groups = rows // LANE
    share = WIN // smp_count
    dma = pltpu.SemaphoreType.DMA
    return pl.pallas_call(
        kernel,
        out_shape=jax.ShapeDtypeStruct((rows, share), jnp.float32),
        in_specs=[pl.BlockSpec(memory_space=pl.ANY), pl.BlockSpec(memory_space=pltpu.VMEM)],
        out_specs=pl.BlockSpec(memory_space=pltpu.VMEM),
        scratch_shapes=[
            pltpu.VMEM((rows, depth), jnp.bfloat16),
            pltpu.VMEM((WIN, depth), jnp.bfloat16),
            pltpu.VMEM((WIN, depth), jnp.bfloat16),
            pltpu.VMEM((SPAN, SPAN, LANE, LANE), jnp.float32),
            pltpu.VMEM((groups, LANE, WIN + LANE), jnp.float32),
            pltpu.VMEM((groups, smp_count, LANE, share), jnp.float32),
            pltpu.VMEM((groups, smp_count, LANE, share), jnp.float32),
            pltpu.VMEM((groups, LANE, share), jnp.float32),
            pltpu.VMEM((2 * groups, LANE), jnp.float32),
            pltpu.VMEM((smp_count - 1, 2 * groups, LANE), jnp.float32),
            pltpu.VMEM((2 * groups, LANE), jnp.float32),
            pltpu.VMEM((2 * groups, LANE), jnp.float32),
            pltpu.VMEM((2 * groups, LANE), jnp.float32),
            dma((groups,)),
            dma((SPAN,)),
            dma((SPAN,)),
            dma((SPAN,)),
            dma((SPAN,)),
            dma((SPAN, SPAN)),
            dma((SPAN, SPAN)),
            dma((smp_count - 1,)),
            dma((smp_count - 1,)),
            dma,
            dma,
            dma,
            dma,
            dma((groups, 3)),
            dma((groups, smp_count)),
            dma((groups,)),
        ],
        compiler_params=pltpu.CompilerParams(
            collective_id=0, has_side_effects=True, vmem_limit_bytes=48 * 1024 * 1024
        ),
    )(dosages, window_end.reshape(groups, LANE))


def solution(mesh):
    return jax.shard_map(
        local,
        mesh=mesh,
        in_specs=(P("var", "smp"), P("var")),
        out_specs=P("var", "smp"),
        check_vma=False,
    )
```

```python
import functools

import jax
import jax.numpy as jnp
from jax import lax
from jax.experimental import pallas as pl
from jax.experimental.pallas import tpu as pltpu
from jax.sharding import PartitionSpec as P

WIN = 512
LANE = 128
SUB = 8
SPAN = WIN // LANE
MESH = pl.DeviceIdType.MESH
NT = (((1,), (1,)), ((), ()))


def kernel(
    x_ref, end_ref, out_ref,
    own, after, before, lent, product, outbox, inbox, relayed, moments, moments_in, final, final_after, final_before,
    load_sem, after_send, after_recv, before_send, before_recv, lent_send, lent_recv, moment_send, moment_recv,
    final_send, final_recv, final_send_right, final_recv_right, band_send, band_recv, relay_recv,
):
    rows, depth = own.shape
    groups = rows // LANE
    var, smp = lax.axis_index("var"), lax.axis_index("smp")
    var_count, smp_count = lax.axis_size("var"), lax.axis_size("smp")
    samples = depth * smp_count
    has_left, has_right = var > 0, var < var_count - 1

    def split_of(boundary):
        between_chips = (boundary + 1) // 2 if var_count == 8 else SPAN // 2
        return jnp.where(lax.rem(boundary, 2) == 0, SPAN, between_chips)

    columns_out = jnp.where(has_left, split_of(var - 1), 0)
    rows_in = jnp.where(has_left, split_of(var - 1), SPAN)
    columns_in = jnp.where(has_right, split_of(var), SPAN)
    rows_out = columns_in

    def peer(step):
        return lax.rem(smp + step, smp_count)

    loads = [
        pltpu.make_async_copy(
            x_ref.at[pl.ds(g * LANE, LANE)], own.at[pl.ds(g * LANE, LANE)], load_sem.at[g]
        )
        for g in range(groups)
    ]
    for load in loads:
        load.start()

    barrier = pltpu.get_barrier_semaphore()
    for step in range(1, smp_count):
        pl.semaphore_signal(barrier, 1, device_id=(var, peer(step)), device_id_type=MESH)

    @pl.when(has_left)
    def _():
        pl.semaphore_signal(barrier, 1, device_id=(var - 1, smp), device_id_type=MESH)

    @pl.when(has_right)
    def _():
        pl.semaphore_signal(barrier, 1, device_id=(var + 1, smp), device_id_type=MESH)

    pl.semaphore_wait(
        barrier, smp_count - 1 + has_left.astype(jnp.int32) + has_right.astype(jnp.int32)
    )

    def after_copy(q):
        return pltpu.make_async_remote_copy(
            src_ref=x_ref.at[pl.ds(q * LANE, LANE)],
            dst_ref=after.at[pl.ds(q * LANE, LANE)],
            send_sem=after_send.at[q],
            recv_sem=after_recv.at[q],
            device_id=(var - 1, smp),
            device_id_type=MESH,
        )

    def before_copy(q):
        return pltpu.make_async_remote_copy(
            src_ref=x_ref.at[pl.ds(rows - WIN + q * LANE, LANE)],
            dst_ref=before.at[pl.ds(q * LANE, LANE)],
            send_sem=before_send.at[q],
            recv_sem=before_recv.at[q],
            device_id=(var + 1, smp),
            device_id_type=MESH,
        )

    def lent_copy(q, c):
        return pltpu.make_async_remote_copy(
            src_ref=lent.at[q, c],
            dst_ref=product.at[groups - SPAN + q, :, pl.ds((c + SPAN - q) * LANE, LANE)],
            send_sem=lent_send.at[q, c],
            recv_sem=lent_recv.at[q, c],
            device_id=(var - 1, smp),
            device_id_type=MESH,
        )

    def final_copy():
        return pltpu.make_async_remote_copy(
            src_ref=final,
            dst_ref=final_after,
            send_sem=final_send,
            recv_sem=final_recv,
            device_id=(var - 1, smp),
            device_id_type=MESH,
        )

    def final_copy_right():
        return pltpu.make_async_remote_copy(
            src_ref=final,
            dst_ref=final_before,
            send_sem=final_send_right,
            recv_sem=final_recv_right,
            device_id=(var + 1, smp),
            device_id_type=MESH,
        )

    for q in range(SPAN):
        @pl.when(q < columns_out)
        def _():
            after_copy(q).start()

        @pl.when(q >= rows_out)
        def _():
            before_copy(q).start()

    for g in range(groups):
        loads[g].wait()

        def add(t, sums):
            tile = own[pl.ds(g * LANE, LANE), pl.ds(pl.multiple_of(t * LANE, LANE), LANE)]
            tile = tile.astype(jnp.float32)
            return sums[0] + tile, sums[1] + tile * tile

        zero = jnp.zeros((LANE, LANE), jnp.float32)
        first, second = lax.fori_loop(0, depth // LANE, add, (zero, zero), unroll=4)
        moments[pl.ds(g, 1), :] = jnp.sum(first.T, axis=0, keepdims=True)
        moments[pl.ds(groups + g, 1), :] = jnp.sum(second.T, axis=0, keepdims=True)

    def moment_copy(step):
        return pltpu.make_async_remote_copy(
            src_ref=moments,
            dst_ref=moments_in.at[step - 1],
            send_sem=moment_send.at[step - 1],
            recv_sem=moment_recv.at[step - 1],
            device_id=(var, peer(step)),
            device_id_type=MESH,
        )

    for step in range(1, smp_count):
        moment_copy(step).start()
    for step in range(1, smp_count):
        moment_copy(step).wait()
    total = moments[...]
    for step in range(1, smp_count):
        total = total + moments_in[step - 1]
    average = total[:groups] / samples
    spread = total[groups:] / samples - average * average
    final[pl.ds(0, groups), :] = average
    final[pl.ds(groups, groups), :] = lax.rsqrt(spread + 1e-06)

    @pl.when(has_left)
    def _():
        final_copy().start()

    @pl.when(has_right)
    def _():
        final_copy_right().start()

    def column(row):
        return jnp.broadcast_to(row, (LANE, LANE)).T

    def standardize(held, g, stats, at_stats):
        shift = column(stats[pl.ds(at_stats, 1), :])
        scale = column(stats[pl.ds(groups + at_stats, 1), :])

        @pl.loop(0, depth // LANE, unroll=4)
        def _(t):
            at = (pl.ds(g * LANE, LANE), pl.ds(pl.multiple_of(t * LANE, LANE), LANE))
            held[at] = ((held[at].astype(jnp.float32) - shift) * scale).astype(jnp.bfloat16)

    inward = jnp.where(smp < smp_count // 2, 1, -1)
    at_end = (smp == 0) | (smp == smp_count - 1)
    far = jnp.where(at_end, smp + 3 * inward, smp + 2 * inward)
    second = jnp.where(at_end, smp + 2 * inward, smp - inward)

    def band_copy(g, slot, share, target, landing, recv_sem):
        return pltpu.make_async_remote_copy(
            src_ref=outbox.at[g, share],
            dst_ref=landing,
            send_sem=band_send.at[g, slot],
            recv_sem=recv_sem,
            device_id=(var, target),
            device_id_type=MESH,
        )

    def direct_copy(g, slot, share):
        return band_copy(g, slot, share, share, inbox.at[g, smp], band_recv.at[g, smp])

    def relay_copy(g):
        return band_copy(g, 2, far, smp + inward, relayed.at[g], relay_recv.at[g])

    def arrival(g, sender):
        return band_copy(g, 0, smp, smp + inward, inbox.at[g, sender], band_recv.at[g, sender])

    def relay_group(g):
        @pl.when(jnp.logical_not(at_end))
        def _():
            relay_copy(g).wait_recv()
            outbox[g, far] = outbox[g, far] + relayed[g]
            direct_copy(g, 2, far).start()

    def finish_group(g):
        width, share = WIN + LANE, WIN // smp_count
        for top in range(0, LANE, SUB):
            value = pltpu.roll(product[g, pl.ds(top, SUB), :], width - 1 - top, 1)
            line = lax.broadcasted_iota(jnp.int32, (SUB, width), 0)
            for bit in range(3):
                moved = pltpu.roll(value, width - (1 << bit), 1)
                value = jnp.where((line >> bit) & 1 == 1, moved, value)
            for part in range(smp_count):
                outbox[g, part, pl.ds(top, SUB), :] = value[:, part * share : (part + 1) * share]

        if g == groups - 1:
            direct_copy(g, 2, far).start()
        else:
            @pl.when(at_end)
            def _():
                relay_copy(g).start()

        direct_copy(g, 0, smp + inward).start()
        direct_copy(g, 1, second).start()

    lane = lax.broadcasted_iota(jnp.int32, (LANE, LANE), 1)
    line = lax.broadcasted_iota(jnp.int32, (LANE, LANE), 0)

    def finalize(g):
        arrival(g, smp + inward).wait_recv()
        arrival(g, second).wait_recv()
        outbox[g, smp] = outbox[g, smp] + inbox[g, smp + inward] + inbox[g, second]

        @pl.when(jnp.logical_not(at_end) | (g == groups - 1))
        def _():
            arrival(g, far).wait_recv()
            outbox[g, smp] = outbox[g, smp] + inbox[g, far]

        end = column(end_ref[pl.ds(g, 1), :].astype(jnp.float32)).astype(jnp.int32)
        index = var * rows + g * LANE + line
        retain = smp * LANE + lane < end - index - 1
        out_ref[pl.ds(g * LANE, LANE), :] = jnp.where(retain, outbox[g, smp] / samples, 0.0)

    def place(value, row, col):
        for i in range(value.shape[0] // LANE):
            for j in range(value.shape[1] // LANE):
                g, c = row + i, col + j - row - i
                if 0 <= c <= SPAN:
                    product[g, :, pl.ds(c * LANE, LANE)] = value[
                        i * LANE : (i + 1) * LANE, j * LANE : (j + 1) * LANE
                    ]

    def dot(left, right):
        return lax.dot_general(left, right, NT, preferred_element_type=jnp.float32)

    scaled = 0
    for g in range(0, groups, 2):
        needed = min(g + SPAN + 2, groups)
        for c in range(scaled, needed):
            standardize(own, c, final, c)
        scaled = needed
        for c in range(g, min(g + SPAN + 2, groups), 2):
            value = dot(own[pl.ds(g * LANE, 2 * LANE), :], own[pl.ds(c * LANE, 2 * LANE), :])
            place(value, g, c)
        for done in range(g, g + 2):
            if done + SPAN < groups:
                finish_group(done)
                if done > 0:
                    relay_group(done - 1)

    @pl.when(has_right)
    def _():
        final_copy().wait_recv()

    @pl.when(jnp.logical_not(has_right))
    def _():
        final_after[...] = jnp.zeros_like(final_after)
        after[...] = jnp.zeros_like(after)

    for q in range(SPAN):
        row = groups - SPAN + q

        @pl.when(q < columns_in)
        def _():
            @pl.when(has_right)
            def _():
                after_copy(q).wait_recv()

            standardize(after, q, final_after, q)
            left = own[pl.ds(row * LANE, (SPAN - q) * LANE), :]
            place(dot(left, after[pl.ds(q * LANE, LANE), :]), row, groups + q)

        relay_group(row - 1)
        if q >= 2:
            @pl.when(columns_in < SPAN)
            def _():
                for g in range(2) if q == 2 else range(2, SPAN + 2):
                    finalize(g)

        for c in range(q + 1):
            @pl.when(c >= columns_in)
            def _():
                lent_copy(q, c).wait_recv()

        finish_group(row)

    @pl.when(has_left)
    def _():
        final_copy_right().wait_recv()

    for q in range(SPAN):
        @pl.when(q >= rows_in)
        def _():
            before_copy(q).wait_recv()
            standardize(before, q, final_before, groups - SPAN + q)
            value = dot(before[pl.ds(q * LANE, LANE), :], own[pl.ds(0, (q + 1) * LANE), :])
            for c in range(q + 1):
                @pl.when(c >= rows_in)
                def _():
                    lent[q, c] = value[:, c * LANE : (c + 1) * LANE]
                    lent_copy(q, c).start()

    @pl.when(columns_in == SPAN)
    def _():
        for g in range(groups - 2):
            finalize(g)

    for g in range(groups - 2, groups):
        finalize(g)

    for g in range(groups):
        for slot in range(3):
            band_copy(
                g, slot, far, smp + inward, relayed.at[g], relay_recv.at[g]
            ).wait_send()

    @pl.when(has_left)
    def _():
        final_copy().wait_send()

    @pl.when(has_right)
    def _():
        final_copy_right().wait_send()

    for q in range(SPAN):
        @pl.when(q < columns_out)
        def _():
            after_copy(q).wait_send()

        @pl.when(q >= rows_out)
        def _():
            before_copy(q).wait_send()

        for c in range(q + 1):
            @pl.when((q >= rows_in) & (c >= rows_in))
            def _():
                lent_copy(q, c).wait_send()


def local(dosages, window_end):
    rows, depth = dosages.shape
    smp_count = lax.axis_size("smp")
    groups = rows // LANE
    share = WIN // smp_count
    dma = pltpu.SemaphoreType.DMA
    return pl.pallas_call(
        kernel,
        out_shape=jax.ShapeDtypeStruct((rows, share), jnp.float32),
        in_specs=[pl.BlockSpec(memory_space=pl.ANY), pl.BlockSpec(memory_space=pltpu.VMEM)],
        out_specs=pl.BlockSpec(memory_space=pltpu.VMEM),
        scratch_shapes=[
            pltpu.VMEM((rows, depth), jnp.bfloat16),
            pltpu.VMEM((WIN, depth), jnp.bfloat16),
            pltpu.VMEM((WIN, depth), jnp.bfloat16),
            pltpu.VMEM((SPAN, SPAN, LANE, LANE), jnp.float32),
            pltpu.VMEM((groups, LANE, WIN + LANE), jnp.float32),
            pltpu.VMEM((groups, smp_count, LANE, share), jnp.float32),
            pltpu.VMEM((groups, smp_count, LANE, share), jnp.float32),
            pltpu.VMEM((groups, LANE, share), jnp.float32),
            pltpu.VMEM((2 * groups, LANE), jnp.float32),
            pltpu.VMEM((smp_count - 1, 2 * groups, LANE), jnp.float32),
            pltpu.VMEM((2 * groups, LANE), jnp.float32),
            pltpu.VMEM((2 * groups, LANE), jnp.float32),
            pltpu.VMEM((2 * groups, LANE), jnp.float32),
            dma((groups,)),
            dma((SPAN,)),
            dma((SPAN,)),
            dma((SPAN,)),
            dma((SPAN,)),
            dma((SPAN, SPAN)),
            dma((SPAN, SPAN)),
            dma((smp_count - 1,)),
            dma((smp_count - 1,)),
            dma,
            dma,
            dma,
            dma,
            dma((groups, 3)),
            dma((groups, smp_count)),
            dma((groups,)),
        ],
        compiler_params=pltpu.CompilerParams(
            collective_id=0, has_side_effects=True, vmem_limit_bytes=48 * 1024 * 1024
        ),
    )(dosages, window_end.reshape(groups, LANE))


def solution(mesh):
    return jax.shard_map(
        local,
        mesh=mesh,
        in_specs=(P("var", "smp"), P("var")),
        out_specs=P("var", "smp"),
        check_vma=False,
    )
```
